32 devices in a mesh: feat: 8 (over z, x), tok: 4 (over y, core).
Axes of the slice: x: 2, y: 2, z: 4, core: 2. Of those that a mesh axis runs over, the one named last changes fastest.
Arguments:
- activations: bfloat16 [512, 8192], P('tok', 'feat'), may hold values from -6 to 6
- w_base: bfloat16 [8192, 8192], P('feat', 'tok'), may hold values from -0.0625 to 0.0625
- blk_vals: bfloat16 [24, 128, 128], P('feat'), may hold values from -0.5 to 0.5
- blk_index: int32 [24, 2], P('feat'), may hold values from 0 to 63, as said below
- blk_count: int32 [8], P('feat'), may hold values from 1 to 3, as said below
- a_down: bfloat16 [8192, 64], P('feat'), may hold values from -0.0625 to 0.0625
- b_up: bfloat16 [64, 8192], P(None, 'feat'), may hold values from -0.75 to 0.75
- grad_out: bfloat16 [512, 8192], P('tok', 'feat'), may hold values from -6 to 6
Outputs:
- projected: bfloat16 [512, 8192], P('tok', 'feat')
- grad_x: bfloat16 [512, 8192], P('tok', 'feat')
- grad_blocks: float32 [24, 128, 128], P('feat')
- grad_a: float32 [8192, 64], P('feat')
- grad_b: float32 [64, 8192], P(None, 'feat')
The draws below stay inside these ranges and needn't reach their ends.
Inputs may be any that keep to these rules, and one draw needn't show every extreme that they name: `blk_index`: column 0 is below 8 and column 1 below 64; both largest values occur in every draw. `blk_count`: some feature shard holds exactly 3 live slots in every draw.
All inputs are finite; a program needn't handle non-finite values.
Results may differ from the reference program's by a relative error of at most 0.014.
Values may be sent and summed in bfloat16 or wider, within the bound.
No kernel may reach another device: no remote copies, remote signals or barrier semaphores. Data moves between devices by JAX's collectives and lax.ppermute only.
A program may use at most 64 MiB of HBM per device.

```python
import jax
import jax.numpy as jnp
from jax import lax

D = 8192
RANK = 64
BLK = 128
SLOTS = 3
TOKENS = 512
SHARDS = 8
RBLK = 8
CBLK = 64
N_FEAT = 8


def draw_blk_index(key, part):
    row_key = jax.random.fold_in(key, 11)
    col_key = jax.random.fold_in(key, 12)
    rows = jax.random.randint(row_key, (SHARDS * SLOTS,), 0, RBLK).astype(jnp.int32)
    cols = jax.random.randint(col_key, (SHARDS * SLOTS,), 0, CBLK).astype(jnp.int32)
    rows = rows.at[0].set(RBLK - 1)
    cols = cols.at[0].set(CBLK - 1)
    return jnp.stack([rows, cols], axis=1)


def draw_blk_count(key, part):
    count_key = jax.random.fold_in(key, 21)
    pick_key = jax.random.fold_in(key, 22)
    counts = jax.random.randint(count_key, (SHARDS,), 1, SLOTS + 1).astype(jnp.int32)
    chosen = jax.random.randint(pick_key, (), 0, SHARDS)
    return counts.at[chosen].set(SLOTS)


def steps_of(key, shape, split, low, high):
    level, own = 1.0, jax.random.fold_in(key, 6)
    for axis_at, parts in split:
        draws = jnp.exp(jax.random.uniform(jax.random.fold_in(own, axis_at), (parts,), jnp.float32, low / len(split), high / len(split)))
        level = level * jnp.repeat(draws, shape[axis_at] // parts).reshape([-1 if axis == axis_at else 1 for axis in range(len(shape))])
    return level


def normal_values(rng, extent, scale, reach, shards=(), held_as=jnp.bfloat16):
    array = jax.random.normal(rng, extent, jnp.float32) * scale
    if len(shards) > 0:
        array = steps_of(rng, extent, shards, -0.22, 0.18) * array
    return jnp.clip(array, min=-reach, max=reach).astype(held_as)


def setup_inputs(seed: int = 0) -> dict:
    streams_of = jax.random.split(jax.random.key(seed), 9)
    return {
        "activations": normal_values(streams_of[0], (TOKENS, D), 1.0, 6.0, ((0, 4), (1, 8))),
        "w_base": normal_values(streams_of[1], (D, D), D ** -0.5, 0.0625, ((0, 8), (1, 4))),
        "blk_vals": normal_values(streams_of[2], (SHARDS * SLOTS, BLK, BLK), BLK ** -0.5, 0.5, ((0, 8),)),
        "blk_index": draw_blk_index(jax.random.fold_in(streams_of[8], 71), 0),
        "blk_count": draw_blk_count(jax.random.fold_in(streams_of[8], 71), 0),
        "a_down": normal_values(streams_of[5], (D, RANK), D ** -0.5, 0.0625, ((0, 8),)),
        "b_up": normal_values(streams_of[6], (RANK, D), RANK ** -0.5, 0.75, ((1, 8),)),
        "grad_out": normal_values(streams_of[7], (TOKENS, D), 1.0, 6.0, ((0, 4), (1, 8))),
    }


def reference(activations, w_base, blk_vals, blk_index, blk_count, a_down, b_up, grad_out):
    tok_rows = activations.shape[0]
    full_width = activations.shape[1]
    shard_width = full_width // N_FEAT
    grad_scale = float(tok_rows) ** -0.5
    backward = jnp.dot(grad_out, w_base.T, preferred_element_type=jnp.float32)
    u_half = jnp.dot(activations, a_down, preferred_element_type=jnp.float32).astype(jnp.bfloat16)
    v_half = jnp.dot(grad_out, b_up.T, preferred_element_type=jnp.float32).astype(jnp.bfloat16)
    summed = jnp.zeros((tok_rows, full_width), jnp.float32)
    block_grads = []
    for owner_idx in range(N_FEAT):
        x_shard = activations[:, owner_idx * shard_width:(owner_idx + 1) * shard_width]
        w_shard = w_base[owner_idx * shard_width:(owner_idx + 1) * shard_width, :]
        partial_value = jnp.dot(x_shard, w_shard, preferred_element_type=jnp.float32)
        for local_idx in range(SLOTS):
            slot_idx = owner_idx * SLOTS + local_idx
            is_live = (local_idx < blk_count[owner_idx]).astype(jnp.float32)
            local_row = (blk_index[slot_idx, 0] * BLK).astype(jnp.int32)
            row_start = (owner_idx * shard_width + blk_index[slot_idx, 0] * BLK).astype(jnp.int32)
            col_start = (blk_index[slot_idx, 1] * BLK).astype(jnp.int32)
            x_cols = lax.dynamic_slice_in_dim(x_shard, local_row, BLK, 1)
            g_cols = lax.dynamic_slice_in_dim(grad_out, col_start, BLK, 1)
            forward_add = jnp.dot(x_cols, blk_vals[slot_idx], preferred_element_type=jnp.float32) * is_live
            current = lax.dynamic_slice_in_dim(partial_value, col_start, BLK, 1)
            partial_value = lax.dynamic_update_slice_in_dim(partial_value, current + forward_add, col_start, 1)
            back_add = jnp.dot(g_cols, blk_vals[slot_idx].T, preferred_element_type=jnp.float32) * is_live
            current = lax.dynamic_slice_in_dim(backward, row_start, BLK, 1)
            backward = lax.dynamic_update_slice_in_dim(backward, current + back_add, row_start, 1)
            block_grads.append(jnp.dot(x_cols.T, g_cols, preferred_element_type=jnp.float32) * is_live * grad_scale)
        summed = summed + partial_value.astype(jnp.bfloat16).astype(jnp.float32)
    projected = (summed + jnp.dot(u_half, b_up, preferred_element_type=jnp.float32)).astype(jnp.bfloat16)
    grad_x = (backward + jnp.dot(v_half, a_down.T, preferred_element_type=jnp.float32)).astype(jnp.bfloat16)
    grad_blocks = jnp.stack(block_grads, axis=0)
    grad_a = jnp.dot(activations.T, v_half, preferred_element_type=jnp.float32) * grad_scale
    grad_b = jnp.dot(u_half.T, grad_out, preferred_element_type=jnp.float32) * grad_scale
    return (projected, grad_x, grad_blocks, grad_a, grad_b)
```

```python
import functools

import jax
import jax.numpy as jnp
from jax import lax
from jax.experimental import pallas as pl
from jax.experimental.pallas import tpu as pltpu
from jax.sharding import PartitionSpec as P

BLK = 128
F32 = jnp.float32
BF16 = jnp.bfloat16
VMEM_BYTES = 48 * 1024 * 1024


def swap(value, axis, mask):
    size = lax.axis_size(axis)
    return lax.ppermute(value, axis, [(i, i ^ mask) for i in range(size)])


def tree_sum(terms):
    while len(terms) > 1:
        terms = [terms[i] + terms[i + 1] for i in range(0, len(terms), 2)]
    return terms[0]


def pick(options, index):
    value = options[0]
    for place in range(1, len(options)):
        value = jnp.where(index == place, options[place], value)
    return value


def added(left, right):
    return (left.astype(F32) + right.astype(F32)).astype(BF16)


def project_kernel(slots, which, scal, x_ref, *refs):
    n_tiles = 2 if which is None else 1
    w_refs, vals_ref = refs[:n_tiles], refs[n_tiles]
    out_refs, acc = refs[n_tiles + 1 : -1], refs[-1]
    step, tile = pl.program_id(0), pl.program_id(1)
    wide, shard = acc.shape[1], x_ref.shape[1]
    far = 1 - step % 2
    held = (1 - step // 2) ^ scal[1] if which is None else which
    for place, w_ref in enumerate(w_refs):

        @pl.when(True if which is not None else held == place)
        def _():
            acc[...] = jnp.dot(x_ref[...], w_ref[...], preferred_element_type=F32)

    first = (2 * (scal[2] ^ held) + (far ^ scal[0])) * shard + tile * wide
    for slot in range(slots):
        local = scal[5 + 2 * slot] * BLK - first

        @pl.when((slot < scal[3]) & (local >= 0) & (local < wide))
        def _():
            columns = pl.ds(pl.multiple_of(local, BLK), BLK)
            x_cols = x_ref[:, pl.ds(pl.multiple_of(scal[4 + 2 * slot] * BLK, BLK), BLK)]
            acc[:, columns] += jnp.dot(x_cols, vals_ref[slot], preferred_element_type=F32)

    for place, out_ref in enumerate(out_refs):

        @pl.when(step == place)
        def _():
            out_ref[...] = acc[...].astype(BF16)


def project(scal, x, tiles, vals, which=None):
    rows, shard = x.shape
    wide = min(512, shard)
    per = shard // wide
    steps = 2 * len(tiles)

    def tile_map(place):
        def index(step, tile, scal):
            if which is not None:
                return 0, ((1 - step) ^ scal[0]) * per + tile
            early = place == (1 ^ scal[1])
            used = early == (step < 2)
            now = ((1 - step % 2) ^ scal[0]) * per + tile
            idle = jnp.where(early, scal[0] * per + per - 1, (1 ^ scal[0]) * per)
            return 0, jnp.where(used, now, idle)

        return index

    def out_map(place):
        return lambda step, tile, scal: (
            0,
            jnp.where(step == place, tile, jnp.where(step < place, 0, per - 1)),
        )

    return pl.pallas_call(
        functools.partial(project_kernel, vals.shape[0], which),
        out_shape=[jax.ShapeDtypeStruct((rows, shard), BF16)] * steps,
        grid_spec=pltpu.PrefetchScalarGridSpec(
            num_scalar_prefetch=1,
            grid=(steps, per),
            in_specs=[pl.BlockSpec((rows, shard), lambda step, tile, scal: (0, 0))]
            + [pl.BlockSpec((shard, wide), tile_map(i)) for i in range(len(tiles))]
            + [pl.BlockSpec(vals.shape, lambda step, tile, scal: (0, 0, 0))],
            out_specs=[pl.BlockSpec((rows, wide), out_map(i)) for i in range(steps)],
            scratch_shapes=[pltpu.VMEM((rows, wide), F32)],
        ),
        compiler_params=pltpu.CompilerParams(
            vmem_limit_bytes=VMEM_BYTES, dimension_semantics=("arbitrary", "arbitrary")
        ),
        cost_estimate=pl.CostEstimate(
            flops=2 * rows * shard * shard * steps,
            bytes_accessed=2 * (shard * shard * steps + rows * shard * (1 + steps)),
            transcendentals=0,
        ),
    )(scal, x, *tiles, vals)


def pull_kernel(slots, groups, scal, *refs):
    x_refs, g_refs, w_refs = refs[:2], refs[2:10], refs[10:12]
    vals_ref, own_ref = refs[12], refs[13]
    rest_refs, blocks_ref, acc = refs[14:-2], refs[-2], refs[-1]
    step = pl.program_id(0)
    shard = acc.shape[1]
    half = acc.shape[0] // 2
    apart, far = step // 2, step % 2
    held = apart ^ scal[1]

    @pl.when(step == 0)
    def _():
        acc[...] = jnp.zeros_like(acc)
        blocks_ref[...] = jnp.zeros_like(blocks_ref)

    first = (2 * (scal[2] ^ held) + (far ^ scal[0])) * shard
    for chunk in range(4):

        @pl.when(step == chunk)
        def _():
            pair = g_refs[2 * chunk : 2 * chunk + 2]
            for place, w_ref in enumerate(w_refs):

                @pl.when(held == place)
                def _():
                    for part, g_ref in enumerate(pair):
                        acc[part * half : (part + 1) * half, :] += lax.dot_general(
                            g_ref[...], w_ref[...], (((1,), (1,)), ((), ())), preferred_element_type=F32
                        )

            for slot in range(slots):
                local = scal[5 + 2 * slot] * BLK - first

                @pl.when((slot < scal[3]) & (local >= 0) & (local < shard))
                def _():
                    columns = pl.ds(pl.multiple_of(local, BLK), BLK)
                    rows = pl.ds(pl.multiple_of(scal[4 + 2 * slot] * BLK, BLK), BLK)
                    for part, g_ref in enumerate(pair):
                        g_cols = g_ref[:, columns]
                        acc[part * half : (part + 1) * half, rows] += lax.dot_general(
                            g_cols, vals_ref[slot], (((1,), (1,)), ((), ())), preferred_element_type=F32
                        )
                        blocks_ref[slot] += lax.dot_general(
                            x_refs[part][:, rows], g_cols, (((0,), (0,)), ((), ())), preferred_element_type=F32
                        )

    @pl.when(step == 3)
    def _():
        rows = acc.shape[0] // groups
        own_ref[...] = acc[:rows, :]
        for place, rest_ref in enumerate(rest_refs):
            rest_ref[...] = acc[(place + 1) * rows : (place + 2) * rows, :].astype(BF16)


def pull(scal, x_pair, chunks, tiles, vals, groups):
    half, shard = x_pair[0].shape
    rows = 2 * half // groups

    def tile_map(place):
        def index(step, scal):
            early = place == scal[1]
            used = early == (step < 2)
            idle = jnp.where(early, 1 ^ scal[0], scal[0])
            return 0, jnp.where(used, (step % 2) ^ scal[0], idle)

        return index

    def whole(shape):
        return pl.BlockSpec(shape, lambda step, scal: (0,) * len(shape))

    return pl.pallas_call(
        functools.partial(pull_kernel, vals.shape[0], groups),
        out_shape=[jax.ShapeDtypeStruct((rows, shard), F32)]
        + [jax.ShapeDtypeStruct((rows, shard), BF16)] * (groups - 1)
        + [jax.ShapeDtypeStruct(vals.shape, F32)],
        grid_spec=pltpu.PrefetchScalarGridSpec(
            num_scalar_prefetch=1,
            grid=(4,),
            in_specs=[whole((half, shard))] * 10
            + [pl.BlockSpec((shard, shard), tile_map(i)) for i in range(2)]
            + [whole(vals.shape)],
            out_specs=[whole((rows, shard))] * groups + [whole(vals.shape)],
            scratch_shapes=[pltpu.VMEM((2 * half, shard), F32)],
        ),
        compiler_params=pltpu.CompilerParams(
            vmem_limit_bytes=VMEM_BYTES, dimension_semantics=("arbitrary",)
        ),
        cost_estimate=pl.CostEstimate(
            flops=2 * 2 * half * shard * shard * 4,
            bytes_accessed=2 * (shard * shard * 4 + half * shard * 12),
            transcendentals=0,
        ),
    )(scal, *x_pair, *chunks, *tiles, vals)


def on_device(activations, w_base, blk_vals, blk_index, blk_count, a_down, b_up, grad_out):
    tok_rows = activations.shape[0]
    n_tok = lax.axis_size("tok")
    grad_scale = float(tok_rows * n_tok) ** (-0.5)
    groups = n_tok // 2
    half_groups = groups // 2
    feat_at, tok_at = lax.axis_index("feat"), lax.axis_index("tok")
    row_at, col_at = feat_at // 2, feat_at % 2
    twist = (row_at ^ tok_at) & 1
    turn = (row_at ^ tok_at) >> 1
    scal = jnp.concatenate(
        [
            jnp.stack([col_at, twist, tok_at]).astype(jnp.int32),
            blk_count,
            blk_index.reshape(-1),
        ]
    )

    def joined(parts):
        return parts[0] if len(parts) == 1 else jnp.concatenate(parts, axis=0)

    cot_seen = [grad_out] + [swap(grad_out, "feat", 4 * step) for step in range(1, groups)]
    other_tile = swap(w_base, "tok", 1)
    x_groups = [activations] + [swap(activations, "tok", 2 * j) for j in range(1, groups)]
    x_near, x_far = joined(x_groups[:half_groups]), joined(x_groups[half_groups:])

    low = jnp.concatenate(
        [
            jnp.dot(activations, a_down, preferred_element_type=F32),
            jnp.dot(grad_out, b_up.T, preferred_element_type=F32),
        ],
        axis=1,
    )
    mask = 1
    while mask < lax.axis_size("feat"):
        low = low + swap(low, "feat", mask)
        mask *= 2
    low = low.astype(BF16)
    rank = a_down.shape[1]
    u_half, v_half = low[:, :rank], low[:, rank:]

    cot_own = [pick(cot_seen, turn)]
    for j in range(1, groups):
        cot_own.append(swap(pick(cot_seen, turn ^ j), "tok", 2 * j))
    g_near, g_far = joined(cot_own[:half_groups]), joined(cot_own[half_groups:])

    sums = []
    for which, tile in enumerate((w_base, other_tile)):
        send, keep = project(scal, x_near, [tile], blk_vals, which)
        sums.append(added(keep, swap(send, "feat", 1)))
    far_11, far_10, far_01, far_00 = project(scal, x_far, [w_base, other_tile], blk_vals)
    far_01 = added(far_01, swap(far_11, "feat", 2))
    far_00 = added(far_00, swap(far_10, "feat", 2))
    near = added(pick(sums, twist), swap(pick(sums, 1 ^ twist), "feat", 2))
    far = added(far_00, swap(far_01, "feat", 1))
    parts = [near[j * tok_rows : (j + 1) * tok_rows] for j in range(half_groups)]
    parts += [far[j * tok_rows : (j + 1) * tok_rows] for j in range(half_groups)]
    parts = [parts[0]] + [swap(parts[j], "tok", 2 * j) for j in range(1, groups)]
    total = pick(parts, turn).astype(F32)
    for step in range(1, groups):
        total = total + swap(pick(parts, turn ^ step), "feat", 4 * step).astype(F32)
    projected = (total + jnp.dot(u_half, b_up, preferred_element_type=F32)).astype(BF16)

    g_near_01, g_far_01 = swap(g_near, "feat", 1), swap(g_far, "feat", 1)
    g_near_10, g_far_10 = swap(g_near, "feat", 2), swap(g_far, "feat", 2)
    g_near_11, g_far_11 = swap(g_near_10, "feat", 1), swap(g_far_01, "feat", 2)
    own, *rest, blocks = pull(
        scal,
        (x_near, x_far),
        (g_near, g_far, g_near_01, g_far_01, g_near_10, g_far_10, g_near_11, g_far_11),
        (w_base, other_tile),
        blk_vals,
        groups,
    )
    for j in range(1, groups):
        own = own + swap(rest[j - 1], "tok", 2 * j).astype(F32)
    grad_x = (own + jnp.dot(v_half, a_down.T, preferred_element_type=F32)).astype(BF16)

    blocks = blocks.astype(BF16)
    up = jnp.dot(u_half.T, grad_out, preferred_element_type=F32)
    v_groups = [v_half] + [swap(v_half, "tok", 2 * j) for j in range(1, groups)]
    down = tree_sum(
        [jnp.dot(x.T, v, preferred_element_type=F32) for x, v in zip(x_groups, v_groups)]
    )
    down = down + swap(down, "tok", 1)
    up = up + swap(up, "tok", 1)
    mask = 2
    while mask < n_tok:
        up = up.astype(BF16)
        up = up.astype(F32) + swap(up, "tok", mask).astype(F32)
        blocks = blocks + swap(blocks, "tok", mask)
        mask *= 2
    blocks = blocks.astype(F32) + swap(blocks, "tok", 1).astype(F32)
    return projected, grad_x, blocks * grad_scale, down * grad_scale, up * grad_scale


def solution(mesh):
    in_specs = (
        P("tok", "feat"),
        P("feat", "tok"),
        P("feat", None, None),
        P("feat", None),
        P("feat"),
        P("feat", None),
        P(None, "feat"),
        P("tok", "feat"),
    )
    out_specs = (
        P("tok", "feat"),
        P("tok", "feat"),
        P("feat", None, None),
        P("feat", None),
        P(None, "feat"),
    )
    return jax.shard_map(
        on_device, mesh=mesh, in_specs=in_specs, out_specs=out_specs, check_vma=False
    )
```

```python
import functools

import jax
import jax.numpy as jnp
from jax import lax
from jax.experimental import pallas as pl
from jax.experimental.pallas import tpu as pltpu
from jax.sharding import PartitionSpec as P

BLK = 128
F32 = jnp.float32
BF16 = jnp.bfloat16
VMEM_BYTES = 32 * 1024 * 1024


def swap(value, axis, mask):
    size = lax.axis_size(axis)
    return lax.ppermute(value, axis, [(i, i ^ mask) for i in range(size)])


def tree_sum(terms):
    while len(terms) > 1:
        terms = [terms[i] + terms[i + 1] for i in range(0, len(terms), 2)]
    return terms[0]


def pick(options, index):
    value = options[0]
    for place in range(1, len(options)):
        value = jnp.where(index == place, options[place], value)
    return value


def after(value, *others):
    return lax.optimization_barrier((value, *others))[0]


def added(left, right):
    return (left.astype(F32) + right.astype(F32)).astype(BF16)


def position():
    feat_at, tok_at = lax.axis_index("feat"), lax.axis_index("tok")
    return feat_at // 2, feat_at % 2, tok_at


def call(kernel, out_shapes, scratch, flops, scalars, arrays):
    space = pl.BlockSpec(memory_space=pltpu.VMEM)
    shapes = [jax.ShapeDtypeStruct(shape, dtype) for shape, dtype in out_shapes]
    size = sum(a.size * a.dtype.itemsize for a in arrays)
    return pl.pallas_call(
        kernel,
        out_shape=shapes,
        in_specs=[pl.BlockSpec(memory_space=pltpu.SMEM)] * len(scalars) + [space] * len(arrays),
        out_specs=[space] * len(shapes),
        scratch_shapes=[pltpu.VMEM(shape, dtype) for shape, dtype in scratch],
        compiler_params=pltpu.CompilerParams(vmem_limit_bytes=VMEM_BYTES),
        cost_estimate=pl.CostEstimate(flops=flops, bytes_accessed=size, transcendentals=0),
    )(*scalars, *arrays)


def for_slots(index_ref, count_ref, slots, first, wide, body):
    for slot in range(slots):
        local = index_ref[1, slot] * BLK - first

        @pl.when((slot < count_ref[0]) & (local >= 0) & (local < wide))
        def _():
            rows = pl.ds(pl.multiple_of(index_ref[0, slot] * BLK, BLK), BLK)
            body(slot, rows, pl.ds(pl.multiple_of(local, BLK), BLK))


def low_kernel(x_ref, g_ref, down_ref, up_ref, out_ref):
    rank = up_ref.shape[0]
    nt = (((1,), (1,)), ((), ()))
    out_ref[:, :rank] = lax.dot_general(x_ref[...], down_ref[...], nt, preferred_element_type=F32)
    out_ref[:, rank:] = lax.dot_general(g_ref[...], up_ref[...], nt, preferred_element_type=F32)


def project(index_ref, count_ref, x_ref, w_ref, vals_ref, acc, held, half):
    shard = x_ref.shape[1]
    columns = pl.ds(pl.multiple_of(half * shard, shard), shard)
    acc[...] = jnp.dot(x_ref[...], w_ref[:, columns], preferred_element_type=F32)

    def body(slot, rows, columns):
        acc[:, columns] += jnp.dot(x_ref[:, rows], vals_ref[slot], preferred_element_type=F32)

    first = (2 * held + half) * shard
    for_slots(index_ref, count_ref, vals_ref.shape[0], first, shard, body)


def own_kernel(index_ref, count_ref, x_ref, w_ref, vals_ref, send_ref, keep_ref, acc):
    _, c, t = position()
    for p, out_ref in ((1, send_ref), (0, keep_ref)):
        project(index_ref, count_ref, x_ref, w_ref, vals_ref, acc, t, p ^ c)
        out_ref[...] = acc[...].astype(BF16)


def rest_kernel(index_ref, count_ref, near_ref, far_ref, own_ref, other_ref, vals_ref, *refs):
    far_refs, near_refs, both, acc, acc_far = refs[:4], refs[4:6], refs[6], refs[7], refs[8]
    r, c, t = position()
    twist = (r ^ t) & 1
    rows = far_ref.shape[0]
    both[:rows, :] = far_ref[...]
    both[rows:, :] = near_ref[...]
    for tile in (1, 0):
        for p in (1, 0):
            x_ref, w_ref, into = (both, other_ref, acc) if tile else (far_ref, own_ref, acc_far)
            project(index_ref, count_ref, x_ref, w_ref, vals_ref, into, t ^ tile, p ^ c)
            if tile:
                near_refs[1 - p][...] = into[rows:, :].astype(BF16)
            for q in (1, 0):

                @pl.when(q ^ twist == tile)
                def _():
                    far_refs[2 * (1 - q) + 1 - p][...] = into[:rows, :].astype(BF16)


def pull(index_ref, count_ref, x_refs, g_refs, w_refs, vals_ref, acc, both, blocks_ref, q, p):
    r, c, t = position()
    held = q ^ ((r ^ t) & 1)
    half = p ^ c
    rows, shard = x_refs[0].shape
    nt = (((1,), (1,)), ((), ()))
    tn = (((0,), (0,)), ((), ()))
    for part in range(2):
        both[part * rows : (part + 1) * rows, :] = g_refs[part][...]
    columns = pl.ds(pl.multiple_of(half * shard, shard), shard)
    for tile, w_ref in enumerate(w_refs):

        @pl.when(held == tile)
        def _():
            acc[...] += lax.dot_general(both[...], w_ref[:, columns], nt, preferred_element_type=F32)

    def body(slot, block_rows, block_columns):
        g_columns = both[:, block_columns]
        acc[:, block_rows] += lax.dot_general(g_columns, vals_ref[slot], nt, preferred_element_type=F32)
        for part in range(2):
            blocks_ref[slot] += lax.dot_general(
                x_refs[part][:, block_rows],
                g_columns[part * rows : (part + 1) * rows],
                tn,
                preferred_element_type=F32,
            )

    first = (2 * (t ^ held) + half) * shard
    for_slots(index_ref, count_ref, vals_ref.shape[0], first, shard, body)


def early_kernel(index_ref, count_ref, *refs):
    x_refs, g_refs, w_refs = refs[:2], refs[2:8], refs[8:10]
    vals_ref, acc, blocks_ref, both = refs[10:]
    acc[...] = jnp.zeros_like(acc)
    blocks_ref[...] = jnp.zeros_like(blocks_ref)
    for place, (q, p) in enumerate(((0, 0), (0, 1), (1, 0))):
        pair = g_refs[2 * place : 2 * place + 2]
        pull(index_ref, count_ref, x_refs, pair, w_refs, vals_ref, acc, both, blocks_ref, q, p)


def late_kernel(index_ref, count_ref, *refs):
    x_refs, g_refs, w_refs = refs[:2], refs[2:4], refs[4:6]
    vals_ref, acc_in, blocks_in = refs[6:9]
    own_ref, *rest_refs, blocks_ref, acc, both = refs[9:]
    acc[...] = acc_in[...]
    blocks_ref[...] = blocks_in[...]
    pull(index_ref, count_ref, x_refs, g_refs, w_refs, vals_ref, acc, both, blocks_ref, 1, 1)
    rows = own_ref.shape[0]
    own_ref[...] = acc[:rows, :]
    for place, rest_ref in enumerate(rest_refs):
        rest_ref[...] = acc[(place + 1) * rows : (place + 2) * rows, :].astype(BF16)


def on_device(activations, w_base, blk_vals, blk_index, blk_count, a_down, b_up, grad_out):
    tok_rows, shard = activations.shape
    n_tok = lax.axis_size("tok")
    grad_scale = float(tok_rows * n_tok) ** (-0.5)
    groups = n_tok // 2
    half_groups = groups // 2
    set_rows = half_groups * tok_rows
    rank = a_down.shape[1]
    r, c, t = position()
    twist = (r ^ t) & 1
    turn = (r ^ t) >> 1
    scalars = (blk_index.T, blk_count)
    product = 2 * set_rows * shard * shard

    def joined(parts):
        return parts[0] if len(parts) == 1 else jnp.concatenate(parts, axis=0)

    other_tile = swap(w_base, "tok", 1)
    x_groups = [activations] + [swap(activations, "tok", 2 * j) for j in range(1, groups)]
    x_near, x_far = joined(x_groups[:half_groups]), joined(x_groups[half_groups:])
    x_pair, tiles = (x_near, x_far), (w_base, other_tile)

    (low,) = call(
        low_kernel,
        [((tok_rows, 2 * rank), F32)],
        [],
        4 * tok_rows * shard * rank,
        (),
        (after(activations, x_far), grad_out, a_down.T, b_up),
    )
    cot_seen = [grad_out] + [swap(grad_out, "feat", 4 * step) for step in range(1, groups)]
    mask = 4
    while mask < lax.axis_size("feat"):
        low = low + swap(low, "feat", mask)
        mask *= 2

    send_own, keep_own = call(
        own_kernel,
        [((set_rows, shard), BF16)] * 2,
        [((set_rows, shard), F32)],
        2 * product,
        scalars,
        (x_near, w_base, blk_vals),
    )
    keep_own = added(keep_own, swap(send_own, "feat", 1))
    far_11, far_10, far_01, far_00, send_other, keep_other = call(
        rest_kernel,
        [((set_rows, shard), BF16)] * 6,
        [((2 * set_rows, shard), BF16), ((2 * set_rows, shard), F32), ((set_rows, shard), F32)],
        6 * product,
        scalars,
        (*x_pair, *tiles, blk_vals),
    )
    low = after(low, far_11)
    low = low + swap(low, "feat", 1)
    keep_other = added(keep_other, swap(send_other, "feat", 1))
    low = after(low, keep_other)
    low = low + swap(low, "feat", 2)
    low = low.astype(BF16)
    u_half, v_half = low[:, :rank], low[:, rank:]
    far_01 = added(far_01, swap(far_11, "feat", 2))
    far_00 = added(far_00, swap(far_10, "feat", 2))
    sums = [keep_own, keep_other]
    near = added(pick(sums, twist), swap(pick(sums, 1 ^ twist), "feat", 2))
    far = added(far_00, swap(far_01, "feat", 1))
    parts = [near[j * tok_rows : (j + 1) * tok_rows] for j in range(half_groups)]
    parts += [far[j * tok_rows : (j + 1) * tok_rows] for j in range(half_groups)]
    parts = [parts[0]] + [swap(parts[j], "tok", 2 * j) for j in range(1, groups)]
    total = pick(parts, turn).astype(F32)
    for step in range(1, groups):
        total = total + swap(pick(parts, turn ^ step), "feat", 4 * step).astype(F32)
    projected = (total + jnp.dot(u_half, b_up, preferred_element_type=F32)).astype(BF16)

    cot_seen = lax.optimization_barrier((*cot_seen, far_11))[:-1]
    cot_own = [pick(cot_seen, turn)]
    for j in range(1, groups):
        cot_own.append(swap(pick(cot_seen, turn ^ j), "tok", 2 * j))
    g_near, g_far = joined(cot_own[:half_groups]), joined(cot_own[half_groups:])
    g_near, g_far = lax.optimization_barrier((g_near, g_far, far_01))[:2]
    g_near_01, g_far_01 = swap(g_near, "feat", 1), swap(g_far, "feat", 1)
    g_near_10, g_far_10 = swap(g_near, "feat", 2), swap(g_far, "feat", 2)
    g_near_11, g_far_11 = swap(g_near_10, "feat", 1), swap(g_far_01, "feat", 2)
    acc, blocks = call(
        early_kernel,
        [((2 * set_rows, shard), F32), (blk_vals.shape, F32)],
        [((2 * set_rows, shard), BF16)],
        6 * product,
        scalars,
        (*x_pair, g_near, g_far, g_near_01, g_far_01, g_near_10, g_far_10, *tiles, blk_vals),
    )
    own, *rest, blocks = call(
        late_kernel,
        [((tok_rows, shard), F32)]
        + [((tok_rows, shard), BF16)] * (groups - 1)
        + [(blk_vals.shape, F32)],
        [((2 * set_rows, shard), F32), ((2 * set_rows, shard), BF16)],
        2 * product,
        scalars,
        (*x_pair, g_near_11, g_far_11, *tiles, blk_vals, acc, blocks),
    )
    for j in range(1, groups):
        own = own + swap(rest[j - 1], "tok", 2 * j).astype(F32)
    grad_x = (own + jnp.dot(v_half, a_down.T, preferred_element_type=F32)).astype(BF16)

    blocks = blocks.astype(BF16)
    up = jnp.dot(u_half.T, grad_out, preferred_element_type=F32)
    v_groups = [v_half] + [swap(v_half, "tok", 2 * j) for j in range(1, groups)]
    down = tree_sum(
        [jnp.dot(x.T, v, preferred_element_type=F32) for x, v in zip(x_groups, v_groups)]
    )
    down = down + swap(down, "tok", 1)
    up = up + swap(up, "tok", 1)
    mask = 2
    while mask < n_tok:
        up = up.astype(BF16)
        up = up.astype(F32) + swap(up, "tok", mask).astype(F32)
        blocks = blocks + swap(blocks, "tok", mask)
        mask *= 2
    blocks = blocks.astype(F32) + swap(blocks, "tok", 1).astype(F32)
    return projected, grad_x, blocks * grad_scale, down * grad_scale, up * grad_scale


def solution(mesh):
    in_specs = (
        P("tok", "feat"),
        P("feat", "tok"),
        P("feat", None, None),
        P("feat", None),
        P("feat"),
        P("feat", None),
        P(None, "feat"),
        P("tok", "feat"),
    )
    out_specs = (
        P("tok", "feat"),
        P("tok", "feat"),
        P("feat", None, None),
        P("feat", None),
        P(None, "feat"),
    )
    return jax.shard_map(
        on_device, mesh=mesh, in_specs=in_specs, out_specs=out_specs, check_vma=False
    )
```

```python
import functools

import jax
import jax.numpy as jnp
from jax import lax
from jax.experimental import pallas as pl
from jax.experimental.pallas import tpu as pltpu
from jax.sharding import PartitionSpec as P

BLK = 128
F32 = jnp.float32
BF16 = jnp.bfloat16
NT = (((1,), (1,)), ((), ()))
TN = (((0,), (0,)), ((), ()))
MIB = 1024 * 1024


def swap(value, axis, mask):
    size = lax.axis_size(axis)
    return lax.ppermute(value, axis, [(i, i ^ mask) for i in range(size)])


def tree_sum(terms):
    while len(terms) > 1:
        terms = [terms[i] + terms[i + 1] for i in range(0, len(terms), 2)]
    return terms[0]


def pick(options, index):
    value = options[0]
    for place in range(1, len(options)):
        value = jnp.where(index == place, options[place], value)
    return value


def after(values, *others):
    return values if not others else lax.optimization_barrier((values, others))[0]


def added(*terms):
    return sum(term.astype(F32) for term in terms).astype(BF16)


def position():
    feat_at, tok_at = lax.axis_index("feat"), lax.axis_index("tok")
    return feat_at // 2, feat_at % 2, tok_at


def call(kernel, limit, weight, out_shapes, scratch, flops, scalars, near, far=(), far_outs=0):
    space, apart = pl.BlockSpec(memory_space=pltpu.VMEM), pl.BlockSpec(memory_space=pltpu.HBM)
    shapes = [jax.ShapeDtypeStruct(shape, dtype) for shape, dtype in out_shapes]
    size = sum(a.size * a.dtype.itemsize for a in (*near, *far))

    def body(*refs):
        sources, refs = refs[: len(scalars)], refs[len(scalars) :]
        if not scalars:
            return kernel(*refs)
        *refs, index_ref, count_ref, sems = refs
        copies = start_copies(list(zip(sources, (index_ref, count_ref))), sems)

        def ready():
            for copy in copies:
                copy.wait()

        return kernel(index_ref, count_ref, ready, *refs)

    held = [pltpu.SMEM(a.shape, a.dtype) for a in scalars]
    return pl.pallas_call(
        body,
        out_shape=shapes,
        in_specs=[apart] * len(scalars) + [space] * len(near) + [apart] * len(far),
        out_specs=[space] * (len(shapes) - far_outs) + [apart] * far_outs,
        scratch_shapes=scratch + held + [pltpu.SemaphoreType.DMA((2,))] * (len(held) > 0),
        compiler_params=pltpu.CompilerParams(vmem_limit_bytes=limit * MIB),
        cost_estimate=pl.CostEstimate(
            flops=int(flops * weight), bytes_accessed=int(size * weight), transcendentals=0
        ),
    )(*scalars, *near, *far)


def start_copies(pairs, sems):
    copies = [pltpu.make_async_copy(src, dst, sems.at[i]) for i, (src, dst) in enumerate(pairs)]
    for copy in copies:
        copy.start()
    return copies


def column_half(half, shard):
    return pl.ds(pl.multiple_of(half * shard, shard), shard)


def for_slots(index_ref, count_ref, slots, first, wide, body):
    for slot in range(slots):
        local = index_ref[1, slot] * BLK - first

        @pl.when((slot < count_ref[0]) & (local >= 0) & (local < wide))
        def _():
            rows = pl.ds(pl.multiple_of(index_ref[0, slot] * BLK, BLK), BLK)
            body(slot, rows, pl.ds(pl.multiple_of(local, BLK), BLK))


def low_kernel(x_in, g_in, down_in, up_in, out_ref, x_ref, g_ref, down_ref, up_ref, sems):
    copies = start_copies([(x_in, x_ref), (down_in, down_ref), (g_in, g_ref), (up_in, up_ref)], sems)
    rank = up_ref.shape[0]
    copies[0].wait()
    copies[1].wait()
    out_ref[:, :rank] = lax.dot_general(x_ref[...], down_ref[...], NT, preferred_element_type=F32)
    copies[2].wait()
    copies[3].wait()
    out_ref[:, rank:] = lax.dot_general(g_ref[...], up_ref[...], NT, preferred_element_type=F32)


def forward_kernel(index_ref, count_ref, ready, far_in, near_in, vals_in, own_in, other_in, *refs):
    outs, (x_ref, w_ref, vals_ref, acc, out_ref, sems, out_sems) = refs[:8], refs[8:]
    r, c, t = position()
    twist = (r ^ t) & 1
    rows, shard = far_in.shape
    places = [(tile, p) for tile in (0, 1) for p in (1, 0)]

    def tile_copy(i):
        tile, p = places[i]
        source = (own_in, other_in)[tile].at[:, column_half(p ^ c, shard)]
        return pltpu.make_async_copy(source, w_ref.at[i], sems.at[i])

    pairs = [(near_in, x_ref.at[rows:, :]), (far_in, x_ref.at[:rows, :]), (vals_in, vals_ref)]
    copies = [pltpu.make_async_copy(s, d, sems.at[4 + i]) for i, (s, d) in enumerate(pairs)]
    for copy in copies:
        copy.start()
    for i in range(len(places)):
        tile_copy(i).start()
    for copy in copies:
        copy.wait()
    ready()
    for i, (tile, p) in enumerate(places):
        tile_copy(i).wait()
        acc[...] = jnp.dot(x_ref[...], w_ref[i], preferred_element_type=F32)

        def body(slot, block_rows, block_columns):
            acc[:, block_columns] += jnp.dot(
                x_ref[:, block_rows], vals_ref[slot], preferred_element_type=F32
            )

        first = (2 * (t ^ tile) + (p ^ c)) * shard
        for_slots(index_ref, count_ref, vals_ref.shape[0], first, shard, body)
        out_ref[i] = acc[...].astype(BF16)
        for q in (1, 0):

            @pl.when(q ^ twist == tile)
            def _():
                at = 2 * (1 - q) + 1 - p
                pltpu.make_async_copy(out_ref.at[i, :rows], outs[at], out_sems.at[2 * i]).start()
                pltpu.make_async_copy(out_ref.at[i, rows:], outs[4 + at], out_sems.at[2 * i + 1]).start()

    for i in range(8):
        pltpu.make_async_copy(out_ref.at[0, :rows], outs[0], out_sems.at[i]).wait()


def start_tile(w_in, target, sem, q, p):
    r, c, t = position()
    half = column_half(p ^ c, target.shape[1])
    for tile in range(2):

        @pl.when(q ^ ((r ^ t) & 1) == tile)
        def _():
            pltpu.make_async_copy(w_in[tile].at[:, half], target, sem).start()

    return pltpu.make_async_copy(w_in[0].at[:, half], target, sem)


def pull(index_ref, count_ref, x_refs, g_refs, vals_ref, w_ref, acc, both, blocks_ref, q, p):
    r, c, t = position()
    rows, shard = x_refs[0].shape
    for part in range(2):
        both[part * rows : (part + 1) * rows, :] = g_refs[part][...]
    acc[...] += lax.dot_general(both[...], w_ref[...], NT, preferred_element_type=F32)

    def body(slot, block_rows, block_columns):
        g_columns = both[:, block_columns]
        acc[:, block_rows] += lax.dot_general(
            g_columns, vals_ref[slot], NT, preferred_element_type=F32
        )
        for part in range(2):
            blocks_ref[slot] += lax.dot_general(
                x_refs[part][:, block_rows],
                g_columns[part * rows : (part + 1) * rows],
                TN,
                preferred_element_type=F32,
            )

    first = (2 * (t ^ q ^ ((r ^ t) & 1)) + (p ^ c)) * shard
    for_slots(index_ref, count_ref, vals_ref.shape[0], first, shard, body)


def early_kernel(index_ref, count_ref, ready, *refs):
    x_refs, g_refs, vals_in, w_in = refs[:2], refs[2:8], refs[8], refs[9:11]
    acc, blocks_ref, last_ref, vals_ref, w_ref, both, sems = refs[11:]
    vals_copy = pltpu.make_async_copy(vals_in, vals_ref, sems.at[4])
    vals_copy.start()
    chunks = ((0, 0), (0, 1), (1, 0))
    copies = [start_tile(w_in, w_ref.at[i], sems.at[i], q, p) for i, (q, p) in enumerate(chunks)]
    last_copy = start_tile(w_in, last_ref, sems.at[3], 1, 1)
    acc[...] = jnp.zeros_like(acc)
    blocks_ref[...] = jnp.zeros_like(blocks_ref)
    vals_copy.wait()
    ready()
    for i, (q, p) in enumerate(chunks):
        copies[i].wait()
        pair = g_refs[2 * i : 2 * i + 2]
        pull(index_ref, count_ref, x_refs, pair, vals_ref, w_ref.at[i], acc, both, blocks_ref, q, p)
    last_copy.wait()


def late_kernel(index_ref, count_ref, ready, *refs):
    x_refs, g_refs, acc_in, blocks_in, vals_ref, w_ref = refs[:2], refs[2:4], *refs[4:8]
    own_ref, *rest_refs, blocks_ref, acc, both = refs[8:]
    acc[...] = acc_in[...]
    blocks_ref[...] = blocks_in[...]
    ready()
    pull(index_ref, count_ref, x_refs, g_refs, vals_ref, w_ref, acc, both, blocks_ref, 1, 1)
    rows = own_ref.shape[0]
    own_ref[...] = acc[:rows, :]
    for place, rest_ref in enumerate(rest_refs):
        rest_ref[...] = acc[(place + 1) * rows : (place + 2) * rows, :].astype(BF16)


def on_device(activations, w_base, blk_vals, blk_index, blk_count, a_down, b_up, grad_out):
    tok_rows, shard = activations.shape
    n_tok = lax.axis_size("tok")
    grad_scale = float(tok_rows * n_tok) ** (-0.5)
    groups = n_tok // 2
    half_groups = groups // 2
    set_rows = half_groups * tok_rows
    rank = a_down.shape[1]
    r, c, t = position()
    turn = (r ^ t) >> 1
    scalars = (blk_index.T, blk_count)
    product = 2 * set_rows * shard * shard
    tall, tile_half = (2 * set_rows, shard), (shard, shard)

    def joined(parts):
        return parts[0] if len(parts) == 1 else jnp.concatenate(parts, axis=0)

    def parted(near, far):
        both = [near[j * tok_rows : (j + 1) * tok_rows] for j in range(half_groups)]
        return both + [far[j * tok_rows : (j + 1) * tok_rows] for j in range(half_groups)]

    other_tile = swap(w_base, "tok", 1)
    x_groups = [activations] + [swap(activations, "tok", 2 * j) for j in range(1, groups)]
    x_near, x_far = joined(x_groups[:half_groups]), joined(x_groups[half_groups:])
    x_pair = (x_near, x_far)
    cot_seen = [grad_out] + [swap(grad_out, "feat", 4 * step) for step in range(1, groups)]

    low_in = (activations, grad_out, a_down.T, b_up)
    (low,) = call(
        low_kernel,
        60,
        1,
        [((tok_rows, 2 * rank), F32)],
        [pltpu.VMEM(a.shape, a.dtype) for a in low_in] + [pltpu.SemaphoreType.DMA((4,))],
        4 * tok_rows * shard * rank,
        (),
        (),
        low_in,
    )
    low = after(low)
    low = low + swap(low, "feat", 1)

    x_far_now = after(x_far, low)

    far_11, far_10, far_01, far_00, near_11, near_10, near_01, near_00 = call(
        forward_kernel,
        60,
        1,
        [((set_rows, shard), BF16)] * 8,
        [
            pltpu.VMEM(tall, BF16),
            pltpu.VMEM((4, *tile_half), BF16),
            pltpu.VMEM(blk_vals.shape, BF16),
            pltpu.VMEM(tall, F32),
            pltpu.VMEM((4, *tall), BF16),
            pltpu.SemaphoreType.DMA((7,)),
            pltpu.SemaphoreType.DMA((8,)),
        ],
        8 * product,
        scalars,
        (),
        (x_far_now, x_near, blk_vals, w_base, other_tile),
        8,
    )
    far_1 = after((far_11, far_10))
    got_far_11, got_far_10 = swap(far_1[0], "feat", 2), swap(far_1[1], "feat", 2)
    got_near_11, got_near_01 = swap(near_11, "feat", 1), swap(near_01, "feat", 1)
    low = after(low)
    low = low + swap(low, "feat", 2)

    cot_seen = after(cot_seen)
    cot_own = [pick(cot_seen, turn)]
    for j in range(1, groups):
        cot_own.append(swap(pick(cot_seen, turn ^ j), "tok", 2 * j))
    g_near, g_far = joined(cot_own[:half_groups]), joined(cot_own[half_groups:])
    far_01 = added(far_01, after(got_far_11, g_near))
    got_far_01 = swap(far_01, "feat", 1)

    near_10 = added(near_10, after(got_near_11, far_01))
    got_near_10 = swap(near_10, "feat", 2)
    far_00 = added(far_00, after(got_far_10, near_10))
    near_00 = added(near_00, after(got_near_01, near_10))
    g_near = after(g_near, far_01)
    g_far = after(g_far, near_10)
    g_far_01, g_near_10 = swap(g_far, "feat", 1), swap(g_near, "feat", 2)
    g_near_01, g_far_10 = swap(g_near, "feat", 1), swap(g_far, "feat", 2)
    low = after(low, g_far)
    mask = 4
    while mask < lax.axis_size("feat"):
        low = low + swap(low, "feat", mask)
        mask *= 2
    far = added(far_00, after(got_far_01, g_far))

    parts = parted(far, far)
    got_parts = {j: swap(parts[j], "tok", 2 * j) for j in range(half_groups, groups)}
    near = added(near_00, after(got_near_10))
    g_near_11 = swap(after(g_near_10, near), "feat", 1)
    g_far_11 = swap(after(g_far_01), "feat", 2)
    parts = parted(near, far)
    got_parts.update({j: swap(parts[j], "tok", 2 * j) for j in range(1, half_groups)})
    parts = [parts[0]] + [got_parts[j] for j in range(1, groups)]
    total = pick(parts, turn).astype(F32)
    sent = [pick(parts, turn ^ step) for step in range(1, groups)]
    got_total = [swap(part, "feat", 4 * step) for step, part in enumerate(sent, 1)]
    low = after(low.astype(BF16))
    u_half, v_half = low[:, :rank], low[:, rank:]
    up = jnp.dot(u_half.T, grad_out, preferred_element_type=F32)
    up = (up + swap(up, "tok", 1)).astype(BF16)
    got_v = [swap(v_half, "tok", 2 * j) for j in range(1, groups)]
    v_groups = [v_half] + after(got_v, near)
    down = tree_sum(
        [jnp.dot(x.T, v, preferred_element_type=F32) for x, v in zip(x_groups, v_groups)]
    )

    acc, blocks, last_tile, vals_seen = call(
        early_kernel,
        32,
        1,
        [(tall, F32), (blk_vals.shape, F32), (tile_half, BF16), (blk_vals.shape, BF16)],
        [
            pltpu.VMEM((3, *tile_half), BF16),
            pltpu.VMEM(tall, BF16),
            pltpu.SemaphoreType.DMA((5,)),
        ],
        6 * product,
        scalars,
        (*x_pair, after(g_near), g_far, g_near_01, g_far_01, g_near_10, g_far_10),
        (blk_vals, w_base, other_tile),
    )
    own, *rest, blocks = call(
        late_kernel,
        32,
        1,
        [((tok_rows, shard), F32)]
        + [((tok_rows, shard), BF16)] * (groups - 1)
        + [(blk_vals.shape, F32)],
        [pltpu.VMEM(tall, F32), pltpu.VMEM(tall, BF16)],
        2 * product,
        scalars,
        (*x_pair, after(g_near_11), g_far_11, acc, blocks, vals_seen, last_tile),
    )
    rest = after(rest)
    got_rest = [swap(rest[j - 1], "tok", 2 * j) for j in range(1, groups)]

    blocks = blocks.astype(BF16)
    down = down + swap(down, "tok", 1)
    mask = 2
    while mask < n_tok:
        up = up.astype(F32) + swap(up.astype(BF16), "tok", mask).astype(F32)
        blocks = blocks + swap(blocks, "tok", mask)
        mask *= 2
    blocks = blocks.astype(F32) + swap(blocks, "tok", 1).astype(F32)

    for got in got_total:
        total = total + got.astype(F32)
    projected = (total + jnp.dot(u_half, b_up, preferred_element_type=F32)).astype(BF16)
    for got in got_rest:
        own = own + got.astype(F32)
    grad_x = (own + jnp.dot(v_half, a_down.T, preferred_element_type=F32)).astype(BF16)
    return projected, grad_x, blocks * grad_scale, down * grad_scale, up * grad_scale


def solution(mesh):
    in_specs = (
        P("tok", "feat"),
        P("feat", "tok"),
        P("feat", None, None),
        P("feat", None),
        P("feat"),
        P("feat", None),
        P(None, "feat"),
        P("tok", "feat"),
    )
    out_specs = (
        P("tok", "feat"),
        P("tok", "feat"),
        P("feat", None, None),
        P("feat", None),
        P(None, "feat"),
    )
    return jax.shard_map(
        on_device, mesh=mesh, in_specs=in_specs, out_specs=out_specs, check_vma=False
    )
```

```python
import functools

import jax
import jax.numpy as jnp
from jax import lax
from jax.experimental import pallas as pl
from jax.experimental.pallas import tpu as pltpu
from jax.sharding import PartitionSpec as P

BLK = 128
F32 = jnp.float32
BF16 = jnp.bfloat16
NT = (((1,), (1,)), ((), ()))
TN = (((0,), (0,)), ((), ()))
MIB = 1024 * 1024


def swap(value, axis, mask):
    size = lax.axis_size(axis)
    return lax.ppermute(value, axis, [(i, i ^ mask) for i in range(size)])


def tree_sum(terms):
    while len(terms) > 1:
        terms = [terms[i] + terms[i + 1] for i in range(0, len(terms), 2)]
    return terms[0]


def pick(options, index):
    value = options[0]
    for place in range(1, len(options)):
        value = jnp.where(index == place, options[place], value)
    return value


def after(values, *others):
    return values if not others else lax.optimization_barrier((values, others))[0]


def added(*terms):
    return sum(term.astype(F32) for term in terms).astype(BF16)


def position():
    feat_at, tok_at = lax.axis_index("feat"), lax.axis_index("tok")
    return feat_at // 2, feat_at % 2, tok_at


def call(kernel, limit, weight, out_shapes, scratch, flops, scalars, near, far=(), far_outs=0):
    space, apart = pl.BlockSpec(memory_space=pltpu.VMEM), pl.BlockSpec(memory_space=pltpu.HBM)
    shapes = [jax.ShapeDtypeStruct(shape, dtype) for shape, dtype in out_shapes]
    size = sum(a.size * a.dtype.itemsize for a in (*near, *far))

    def body(*refs):
        sources, refs = refs[: len(scalars)], refs[len(scalars) :]
        if not scalars:
            return kernel(*refs)
        *refs, index_ref, count_ref, sems = refs
        copies = start_copies(list(zip(sources, (index_ref, count_ref))), sems)

        def ready():
            for copy in copies:
                copy.wait()

        return kernel(index_ref, count_ref, ready, *refs)

    held = [pltpu.SMEM(a.shape, a.dtype) for a in scalars]
    return pl.pallas_call(
        body,
        out_shape=shapes,
        in_specs=[apart] * len(scalars) + [space] * len(near) + [apart] * len(far),
        out_specs=[space] * (len(shapes) - far_outs) + [apart] * far_outs,
        scratch_shapes=scratch + held + [pltpu.SemaphoreType.DMA((2,))] * (len(held) > 0),
        compiler_params=pltpu.CompilerParams(vmem_limit_bytes=limit * MIB),
        cost_estimate=pl.CostEstimate(
            flops=int(flops * weight), bytes_accessed=int(size * weight), transcendentals=0
        ),
    )(*scalars, *near, *far)


def start_copies(pairs, sems):
    copies = [pltpu.make_async_copy(src, dst, sems.at[i]) for i, (src, dst) in enumerate(pairs)]
    for copy in copies:
        copy.start()
    return copies


def column_half(half, shard):
    return pl.ds(pl.multiple_of(half * shard, shard), shard)


def for_slots(index_ref, count_ref, slots, first, wide, body):
    for slot in range(slots):
        local = index_ref[1, slot] * BLK - first

        @pl.when((slot < count_ref[0]) & (local >= 0) & (local < wide))
        def _():
            rows = pl.ds(pl.multiple_of(index_ref[0, slot] * BLK, BLK), BLK)
            body(slot, rows, pl.ds(pl.multiple_of(local, BLK), BLK))


def low_kernel(x_in, g_in, down_in, up_in, out_ref, x_ref, g_ref, down_ref, up_ref, sems):
    copies = start_copies([(x_in, x_ref), (down_in, down_ref), (g_in, g_ref), (up_in, up_ref)], sems)
    rank = up_ref.shape[0]
    copies[0].wait()
    copies[1].wait()
    out_ref[:, :rank] = lax.dot_general(x_ref[...], down_ref[...], NT, preferred_element_type=F32)
    copies[2].wait()
    copies[3].wait()
    out_ref[:, rank:] = lax.dot_general(g_ref[...], up_ref[...], NT, preferred_element_type=F32)


def forward_kernel(index_ref, count_ref, ready, far_in, near_in, vals_in, own_in, other_in, *refs):
    outs, (x_ref, w_ref, vals_ref, acc, out_ref, sems, out_sems) = refs[:8], refs[8:]
    r, c, t = position()
    twist = (r ^ t) & 1
    rows, shard = far_in.shape
    places = [(tile, p) for tile in (0, 1) for p in (1, 0)]

    def tile_copy(i):
        tile, p = places[i]
        source = (own_in, other_in)[tile].at[:, column_half(p ^ c, shard)]
        return pltpu.make_async_copy(source, w_ref.at[i], sems.at[i])

    pairs = [(near_in, x_ref.at[rows:, :]), (far_in, x_ref.at[:rows, :]), (vals_in, vals_ref)]
    copies = [pltpu.make_async_copy(s, d, sems.at[4 + i]) for i, (s, d) in enumerate(pairs)]
    for copy in copies:
        copy.start()
    for i in range(len(places)):
        tile_copy(i).start()
    for copy in copies:
        copy.wait()
    ready()
    for i, (tile, p) in enumerate(places):
        tile_copy(i).wait()
        acc[...] = jnp.dot(x_ref[...], w_ref[i], preferred_element_type=F32)

        def body(slot, block_rows, block_columns):
            acc[:, block_columns] += jnp.dot(
                x_ref[:, block_rows], vals_ref[slot], preferred_element_type=F32
            )

        first = (2 * (t ^ tile) + (p ^ c)) * shard
        for_slots(index_ref, count_ref, vals_ref.shape[0], first, shard, body)
        out_ref[i] = acc[...].astype(BF16)
        for q in (1, 0):

            @pl.when(q ^ twist == tile)
            def _():
                at = 2 * (1 - q) + 1 - p
                pltpu.make_async_copy(out_ref.at[i, :rows], outs[at], out_sems.at[2 * i]).start()
                pltpu.make_async_copy(out_ref.at[i, rows:], outs[4 + at], out_sems.at[2 * i + 1]).start()

    for i in range(8):
        pltpu.make_async_copy(out_ref.at[0, :rows], outs[0], out_sems.at[i]).wait()


def start_tile(w_in, target, sem, q, p):
    r, c, t = position()
    half = column_half(p ^ c, target.shape[1])
    for tile in range(2):

        @pl.when(q ^ ((r ^ t) & 1) == tile)
        def _():
            pltpu.make_async_copy(w_in[tile].at[:, half], target, sem).start()

    return pltpu.make_async_copy(w_in[0].at[:, half], target, sem)


def pull(index_ref, count_ref, x_refs, g_ref, vals_ref, w_ref, acc, blocks_ref, q, p):
    r, c, t = position()
    rows, shard = x_refs[0].shape
    acc[...] += lax.dot_general(g_ref[...], w_ref[...], NT, preferred_element_type=F32)

    def body(slot, block_rows, block_columns):
        g_columns = g_ref[:, block_columns]
        acc[:, block_rows] += lax.dot_general(
            g_columns, vals_ref[slot], NT, preferred_element_type=F32
        )
        for part, x_ref in enumerate(x_refs):
            blocks_ref[slot] += lax.dot_general(
                x_ref[:, block_rows],
                g_columns[part * rows : (part + 1) * rows],
                TN,
                preferred_element_type=F32,
            )

    first = (2 * (t ^ q ^ ((r ^ t) & 1)) + (p ^ c)) * shard
    for_slots(index_ref, count_ref, vals_ref.shape[0], first, shard, body)


def early_kernel(index_ref, count_ref, ready, *refs):
    x_refs, g_refs, vals_in, w_in = refs[:2], refs[2:8], refs[8], refs[9:11]
    near_ref, far_ref, blocks_ref, last_ref, vals_ref, w_ref, both, acc, sems = refs[11:]
    vals_copy = pltpu.make_async_copy(vals_in, vals_ref, sems.at[4])
    vals_copy.start()
    chunks = ((0, 0), (0, 1), (1, 0))
    copies = [start_tile(w_in, w_ref.at[i], sems.at[i], q, p) for i, (q, p) in enumerate(chunks)]
    last_copy = start_tile(w_in, last_ref, sems.at[3], 1, 1)
    acc[...] = jnp.zeros_like(acc)
    blocks_ref[...] = jnp.zeros_like(blocks_ref)
    vals_copy.wait()
    ready()
    rows = near_ref.shape[0]
    for i, (q, p) in enumerate(chunks):
        for part in range(2):
            both[part * rows : (part + 1) * rows, :] = g_refs[2 * i + part][...]
        copies[i].wait()
        pull(index_ref, count_ref, x_refs, both, vals_ref, w_ref.at[i], acc, blocks_ref, q, p)
    near_ref[...] = acc[:rows, :]
    far_ref[...] = acc[rows:, :]
    last_copy.wait()


def late_kernel(index_ref, count_ref, ready, x_ref, g_ref, acc_in, blocks_in, vals_ref, w_ref, *refs):
    *out_refs, blocks_ref, acc = refs
    acc[...] = acc_in[...]
    blocks_ref[...] = blocks_in[...]
    ready()
    pull(index_ref, count_ref, (x_ref,), g_ref, vals_ref, w_ref, acc, blocks_ref, 1, 1)
    rows = out_refs[0].shape[0]
    for place, out_ref in enumerate(out_refs):
        out_ref[...] = acc[place * rows : (place + 1) * rows, :].astype(out_ref.dtype)


def on_device(activations, w_base, blk_vals, blk_index, blk_count, a_down, b_up, grad_out):
    tok_rows, shard = activations.shape
    n_tok = lax.axis_size("tok")
    grad_scale = float(tok_rows * n_tok) ** (-0.5)
    groups = n_tok // 2
    half_groups = groups // 2
    set_rows = half_groups * tok_rows
    rank = a_down.shape[1]
    r, c, t = position()
    turn = (r ^ t) >> 1
    scalars = (blk_index.T, blk_count)
    product = 2 * set_rows * shard * shard
    tall, tile_half = (2 * set_rows, shard), (shard, shard)

    def joined(parts):
        return parts[0] if len(parts) == 1 else jnp.concatenate(parts, axis=0)

    def parted(near, far):
        both = [near[j * tok_rows : (j + 1) * tok_rows] for j in range(half_groups)]
        return both + [far[j * tok_rows : (j + 1) * tok_rows] for j in range(half_groups)]

    other_tile = swap(w_base, "tok", 1)
    x_groups = [activations] + [swap(activations, "tok", 2 * j) for j in range(1, groups)]
    x_near, x_far = joined(x_groups[:half_groups]), joined(x_groups[half_groups:])
    x_pair = (x_near, x_far)
    cot_seen = [grad_out] + [swap(grad_out, "feat", 4 * step) for step in range(1, groups)]

    low_in = (activations, grad_out, a_down.T, b_up)
    (low,) = call(
        low_kernel,
        60,
        1,
        [((tok_rows, 2 * rank), F32)],
        [pltpu.VMEM(a.shape, a.dtype) for a in low_in] + [pltpu.SemaphoreType.DMA((4,))],
        4 * tok_rows * shard * rank,
        (),
        (),
        low_in,
    )
    low = after(low)
    low = low + swap(low, "feat", 1)

    x_far_now = after(x_far, low)

    far_11, far_10, far_01, far_00, near_11, near_10, near_01, near_00 = call(
        forward_kernel,
        60,
        1,
        [((set_rows, shard), BF16)] * 8,
        [
            pltpu.VMEM(tall, BF16),
            pltpu.VMEM((4, *tile_half), BF16),
            pltpu.VMEM(blk_vals.shape, BF16),
            pltpu.VMEM(tall, F32),
            pltpu.VMEM((4, *tall), BF16),
            pltpu.SemaphoreType.DMA((7,)),
            pltpu.SemaphoreType.DMA((8,)),
        ],
        8 * product,
        scalars,
        (),
        (x_far_now, x_near, blk_vals, w_base, other_tile),
        8,
    )
    far_1 = after((far_11, far_10))
    got_far_11, got_far_10 = swap(far_1[0], "feat", 2), swap(far_1[1], "feat", 2)
    got_near_11, got_near_01 = swap(near_11, "feat", 1), swap(near_01, "feat", 1)
    low = after(low)
    low = low + swap(low, "feat", 2)

    cot_seen = after(cot_seen)
    cot_own = [pick(cot_seen, turn)]
    for j in range(1, groups):
        cot_own.append(swap(pick(cot_seen, turn ^ j), "tok", 2 * j))
    g_near, g_far = joined(cot_own[:half_groups]), joined(cot_own[half_groups:])
    far_01 = added(far_01, after(got_far_11, g_near))
    got_far_01 = swap(far_01, "feat", 1)

    near_10 = added(near_10, after(got_near_11, far_01))
    got_near_10 = swap(near_10, "feat", 2)
    far_00 = added(far_00, after(got_far_10, near_10))
    near_00 = added(near_00, after(got_near_01, near_10))
    g_near = after(g_near, far_01)
    g_far = after(g_far, near_10)
    g_far_01, g_near_10 = swap(g_far, "feat", 1), swap(g_near, "feat", 2)
    g_near_01, g_far_10 = swap(g_near, "feat", 1), swap(g_far, "feat", 2)
    low = after(low, g_far)
    mask = 4
    while mask < lax.axis_size("feat"):
        low = low + swap(low, "feat", mask)
        mask *= 2
    far = added(far_00, after(got_far_01, g_near, g_far))

    parts = parted(far, far)
    got_parts = {j: swap(parts[j], "tok", 2 * j) for j in range(half_groups, groups)}
    near = added(near_00, after(got_near_10))
    g_near_11 = swap(after(g_near_10, near), "feat", 1)
    g_far_11 = swap(after(g_far_01), "feat", 2)
    parts = parted(near, far)
    got_parts.update({j: swap(parts[j], "tok", 2 * j) for j in range(1, half_groups)})
    parts = [parts[0]] + [got_parts[j] for j in range(1, groups)]
    total = pick(parts, turn).astype(F32)
    sent = [pick(parts, turn ^ step) for step in range(1, groups)]
    got_total = [swap(part, "feat", 4 * step) for step, part in enumerate(sent, 1)]
    low = after(low.astype(BF16))
    u_half, v_half = low[:, :rank], low[:, rank:]
    up = jnp.dot(u_half.T, grad_out, preferred_element_type=F32)
    up = (up + after(swap(up, "tok", 1))).astype(BF16)
    got_v = [swap(v_half, "tok", 2 * j) for j in range(1, groups)]
    v_groups = [v_half] + after(got_v, near)
    down = tree_sum(
        [jnp.dot(x.T, v, preferred_element_type=F32) for x, v in zip(x_groups, v_groups)]
    )

    short = (set_rows, shard)
    acc_near, acc_far, blocks, last_tile, vals_seen = call(
        early_kernel,
        32,
        1,
        [(short, F32)] * 2 + [(blk_vals.shape, F32), (tile_half, BF16), (blk_vals.shape, BF16)],
        [
            pltpu.VMEM((3, *tile_half), BF16),
            pltpu.VMEM(tall, BF16),
            pltpu.VMEM(tall, F32),
            pltpu.SemaphoreType.DMA((5,)),
        ],
        6 * product,
        scalars,
        (*x_pair, after(g_near), g_far, g_near_01, g_far_01, g_near_10, g_far_10),
        (blk_vals, w_base, other_tile),
    )
    piece = (tok_rows, shard)
    *rest_far, blocks = call(
        late_kernel,
        32,
        0.01,
        [(piece, BF16)] * half_groups + [(blk_vals.shape, F32)],
        [pltpu.VMEM(short, F32)],
        product,
        scalars,
        (x_far, after(g_far_11), acc_far, blocks, vals_seen, last_tile),
    )
    own, *rest, blocks = call(
        late_kernel,
        32,
        0.01,
        [(piece, F32)] + [(piece, BF16)] * (half_groups - 1) + [(blk_vals.shape, F32)],
        [pltpu.VMEM(short, F32)],
        product,
        scalars,
        (x_near, g_near_11, acc_near, blocks, vals_seen, last_tile),
    )
    rest = [*rest, *rest_far]
    rest = after(rest)
    got_rest = [swap(rest[j - 1], "tok", 2 * j) for j in range(1, groups)]

    blocks = blocks.astype(BF16)
    down = down + after(swap(down, "tok", 1))
    mask = 2
    while mask < n_tok:
        up = up.astype(F32) + after(swap(up.astype(BF16), "tok", mask)).astype(F32)
        blocks = blocks + swap(blocks, "tok", mask)
        mask *= 2
    blocks = blocks.astype(F32) + swap(blocks, "tok", 1).astype(F32)

    for got in got_total:
        total = total + got.astype(F32)
    projected = (total + jnp.dot(u_half, b_up, preferred_element_type=F32)).astype(BF16)
    for got in got_rest:
        own = own + got.astype(F32)
    grad_x = (own + jnp.dot(v_half, a_down.T, preferred_element_type=F32)).astype(BF16)
    return projected, grad_x, blocks * grad_scale, down * grad_scale, up * grad_scale


def solution(mesh):
    in_specs = (
        P("tok", "feat"),
        P("feat", "tok"),
        P("feat", None, None),
        P("feat", None),
        P("feat"),
        P("feat", None),
        P(None, "feat"),
        P("tok", "feat"),
    )
    out_specs = (
        P("tok", "feat"),
        P("tok", "feat"),
        P("feat", None, None),
        P("feat", None),
        P(None, "feat"),
    )
    return jax.shard_map(
        on_device, mesh=mesh, in_specs=in_specs, out_specs=out_specs, check_vma=False
    )
```

```python
import functools

import jax
import jax.numpy as jnp
from jax import lax
from jax.experimental import pallas as pl
from jax.experimental.pallas import tpu as pltpu
from jax.sharding import PartitionSpec as P

BLK = 128
F32 = jnp.float32
BF16 = jnp.bfloat16
NT = (((1,), (1,)), ((), ()))
TN = (((0,), (0,)), ((), ()))
MIB = 1024 * 1024


def swap(value, axis, mask):
    size = lax.axis_size(axis)
    return lax.ppermute(value, axis, [(i, i ^ mask) for i in range(size)])


def tree_sum(terms):
    while len(terms) > 1:
        terms = [terms[i] + terms[i + 1] for i in range(0, len(terms), 2)]
    return terms[0]


def pick(options, index):
    value = options[0]
    for place in range(1, len(options)):
        value = jnp.where(index == place, options[place], value)
    return value


def after(values, *others):
    return values if not others else lax.optimization_barrier((values, others))[0]


def added(*terms):
    return sum(term.astype(F32) for term in terms).astype(BF16)


def position():
    feat_at, tok_at = lax.axis_index("feat"), lax.axis_index("tok")
    return feat_at // 2, feat_at % 2, tok_at


def call(kernel, limit, weight, out_shapes, scratch, flops, scalars, near, far=(), far_outs=0):
    space, apart = pl.BlockSpec(memory_space=pltpu.VMEM), pl.BlockSpec(memory_space=pltpu.HBM)
    shapes = [jax.ShapeDtypeStruct(shape, dtype) for shape, dtype in out_shapes]
    size = sum(a.size * a.dtype.itemsize for a in (*near, *far))

    def body(*refs):
        sources, refs = refs[: len(scalars)], refs[len(scalars) :]
        if not scalars:
            return kernel(*refs)
        *refs, index_ref, count_ref, sems = refs
        copies = start_copies(list(zip(sources, (index_ref, count_ref))), sems)

        def ready():
            for copy in copies:
                copy.wait()

        return kernel(index_ref, count_ref, ready, *refs)

    held = [pltpu.SMEM(a.shape, a.dtype) for a in scalars]
    return pl.pallas_call(
        body,
        out_shape=shapes,
        in_specs=[apart] * len(scalars) + [space] * len(near) + [apart] * len(far),
        out_specs=[space] * (len(shapes) - far_outs) + [apart] * far_outs,
        scratch_shapes=scratch + held + [pltpu.SemaphoreType.DMA((2,))] * (len(held) > 0),
        compiler_params=pltpu.CompilerParams(vmem_limit_bytes=limit * MIB),
        cost_estimate=pl.CostEstimate(
            flops=int(flops * weight), bytes_accessed=int(size * weight), transcendentals=0
        ),
    )(*scalars, *near, *far)


def start_copies(pairs, sems):
    copies = [pltpu.make_async_copy(src, dst, sems.at[i]) for i, (src, dst) in enumerate(pairs)]
    for copy in copies:
        copy.start()
    return copies


def column_half(half, shard):
    return pl.ds(pl.multiple_of(half * shard, shard), shard)


def for_slots(index_ref, count_ref, slots, first, wide, body):
    for slot in range(slots):
        local = index_ref[1, slot] * BLK - first

        @pl.when((slot < count_ref[0]) & (local >= 0) & (local < wide))
        def _():
            rows = pl.ds(pl.multiple_of(index_ref[0, slot] * BLK, BLK), BLK)
            body(slot, rows, pl.ds(pl.multiple_of(local, BLK), BLK))


def low_kernel(x_in, g_in, down_in, up_in, out_ref, x_ref, g_ref, down_ref, up_ref, sems):
    copies = start_copies([(x_in, x_ref), (down_in, down_ref), (g_in, g_ref), (up_in, up_ref)], sems)
    rank = up_ref.shape[0]
    copies[0].wait()
    copies[1].wait()
    out_ref[:, :rank] = lax.dot_general(x_ref[...], down_ref[...], NT, preferred_element_type=F32)
    copies[2].wait()
    copies[3].wait()
    out_ref[:, rank:] = lax.dot_general(g_ref[...], up_ref[...], NT, preferred_element_type=F32)


def forward_kernel(index_ref, count_ref, ready, far_in, near_in, vals_in, own_in, other_in, *refs):
    outs, (x_ref, w_ref, vals_ref, acc, out_ref, sems, out_sems) = refs[:8], refs[8:]
    r, c, t = position()
    twist = (r ^ t) & 1
    rows, shard = far_in.shape
    places = [(tile, p) for tile in (0, 1) for p in (1, 0)]

    def tile_copy(i):
        tile, p = places[i]
        source = (own_in, other_in)[tile].at[:, column_half(p ^ c, shard)]
        return pltpu.make_async_copy(source, w_ref.at[i], sems.at[i])

    pairs = [(near_in, x_ref.at[rows:, :]), (far_in, x_ref.at[:rows, :]), (vals_in, vals_ref)]
    copies = [pltpu.make_async_copy(s, d, sems.at[4 + i]) for i, (s, d) in enumerate(pairs)]
    for copy in copies:
        copy.start()
    for i in range(len(places)):
        tile_copy(i).start()
    for copy in copies:
        copy.wait()
    ready()
    for i, (tile, p) in enumerate(places):
        tile_copy(i).wait()
        acc[...] = jnp.dot(x_ref[...], w_ref[i], preferred_element_type=F32)

        def body(slot, block_rows, block_columns):
            acc[:, block_columns] += jnp.dot(
                x_ref[:, block_rows], vals_ref[slot], preferred_element_type=F32
            )

        first = (2 * (t ^ tile) + (p ^ c)) * shard
        for_slots(index_ref, count_ref, vals_ref.shape[0], first, shard, body)
        out_ref[i] = acc[...].astype(BF16)
        for q in (1, 0):

            @pl.when(q ^ twist == tile)
            def _():
                at = 2 * (1 - q) + 1 - p
                pltpu.make_async_copy(out_ref.at[i, :rows], outs[at], out_sems.at[2 * i]).start()
                pltpu.make_async_copy(out_ref.at[i, rows:], outs[4 + at], out_sems.at[2 * i + 1]).start()

    for i in range(8):
        pltpu.make_async_copy(out_ref.at[0, :rows], outs[0], out_sems.at[i]).wait()


def start_tile(w_in, target, sem, q, p):
    r, c, t = position()
    half = column_half(p ^ c, target.shape[1])
    for tile in range(2):

        @pl.when(q ^ ((r ^ t) & 1) == tile)
        def _():
            pltpu.make_async_copy(w_in[tile].at[:, half], target, sem).start()

    return pltpu.make_async_copy(w_in[0].at[:, half], target, sem)


def pull(index_ref, count_ref, x_refs, g_ref, vals_ref, w_ref, acc, blocks_ref, q, p):
    r, c, t = position()
    rows, shard = x_refs[0].shape
    acc[...] += lax.dot_general(g_ref[...], w_ref[...], NT, preferred_element_type=F32)

    def body(slot, block_rows, block_columns):
        g_columns = g_ref[:, block_columns]
        acc[:, block_rows] += lax.dot_general(
            g_columns, vals_ref[slot], NT, preferred_element_type=F32
        )
        for part, x_ref in enumerate(x_refs):
            blocks_ref[slot] += lax.dot_general(
                x_ref[:, block_rows],
                g_columns[part * rows : (part + 1) * rows],
                TN,
                preferred_element_type=F32,
            )

    first = (2 * (t ^ q ^ ((r ^ t) & 1)) + (p ^ c)) * shard
    for_slots(index_ref, count_ref, vals_ref.shape[0], first, shard, body)


def early_kernel(index_ref, count_ref, ready, *refs):
    x_refs, g_refs, vals_in, w_in = refs[:2], refs[2:8], refs[8], refs[9:11]
    near_ref, far_ref, blocks_ref, last_ref, vals_ref, w_ref, both, acc, sems = refs[11:]
    vals_copy = pltpu.make_async_copy(vals_in, vals_ref, sems.at[4])
    vals_copy.start()
    chunks = ((0, 0), (0, 1), (1, 0))
    copies = [start_tile(w_in, w_ref.at[i], sems.at[i], q, p) for i, (q, p) in enumerate(chunks)]
    last_copy = start_tile(w_in, last_ref, sems.at[3], 1, 1)
    acc[...] = jnp.zeros_like(acc)
    blocks_ref[...] = jnp.zeros_like(blocks_ref)
    vals_copy.wait()
    ready()
    rows = near_ref.shape[0]
    for i, (q, p) in enumerate(chunks):
        for part in range(2):
            both[part * rows : (part + 1) * rows, :] = g_refs[2 * i + part][...]
        copies[i].wait()
        pull(index_ref, count_ref, x_refs, both, vals_ref, w_ref.at[i], acc, blocks_ref, q, p)
    near_ref[...] = acc[:rows, :]
    far_ref[...] = acc[rows:, :]
    last_copy.wait()


def late_kernel(index_ref, count_ref, ready, x_ref, g_ref, acc_in, blocks_in, vals_ref, w_ref, *refs):
    *out_refs, blocks_ref, acc = refs
    acc[...] = acc_in[...]
    blocks_ref[...] = blocks_in[...]
    ready()
    pull(index_ref, count_ref, (x_ref,), g_ref, vals_ref, w_ref, acc, blocks_ref, 1, 1)
    rows = out_refs[0].shape[0]
    for place, out_ref in enumerate(out_refs):
        out_ref[...] = acc[place * rows : (place + 1) * rows, :].astype(out_ref.dtype)


def on_device(activations, w_base, blk_vals, blk_index, blk_count, a_down, b_up, grad_out):
    tok_rows, shard = activations.shape
    n_tok = lax.axis_size("tok")
    grad_scale = float(tok_rows * n_tok) ** (-0.5)
    groups = n_tok // 2
    half_groups = groups // 2
    set_rows = half_groups * tok_rows
    rank = a_down.shape[1]
    r, c, t = position()
    turn = (r ^ t) >> 1
    scalars = (blk_index.T, blk_count)
    product = 2 * set_rows * shard * shard
    tall, tile_half = (2 * set_rows, shard), (shard, shard)

    def joined(parts):
        return parts[0] if len(parts) == 1 else jnp.concatenate(parts, axis=0)

    def parted(near, far):
        both = [near[j * tok_rows : (j + 1) * tok_rows] for j in range(half_groups)]
        return both + [far[j * tok_rows : (j + 1) * tok_rows] for j in range(half_groups)]

    other_tile = swap(w_base, "tok", 1)
    x_groups = [activations] + [swap(activations, "tok", 2 * j) for j in range(1, groups)]
    x_near, x_far = joined(x_groups[:half_groups]), joined(x_groups[half_groups:])
    x_pair = (x_near, x_far)
    cot_seen = [grad_out] + [swap(grad_out, "feat", 4 * step) for step in range(1, groups)]

    low_in = (activations, grad_out, a_down.T, b_up)
    (low,) = call(
        low_kernel,
        60,
        1,
        [((tok_rows, 2 * rank), F32)],
        [pltpu.VMEM(a.shape, a.dtype) for a in low_in] + [pltpu.SemaphoreType.DMA((4,))],
        4 * tok_rows * shard * rank,
        (),
        (),
        low_in,
    )
    low = after(low)
    low = low + swap(low, "feat", 1)

    x_far_now = after(x_far, low)

    far_11, far_10, far_01, far_00, near_11, near_10, near_01, near_00 = call(
        forward_kernel,
        60,
        1,
        [((set_rows, shard), BF16)] * 8,
        [
            pltpu.VMEM(tall, BF16),
            pltpu.VMEM((4, *tile_half), BF16),
            pltpu.VMEM(blk_vals.shape, BF16),
            pltpu.VMEM(tall, F32),
            pltpu.VMEM((4, *tall), BF16),
            pltpu.SemaphoreType.DMA((7,)),
            pltpu.SemaphoreType.DMA((8,)),
        ],
        8 * product,
        scalars,
        (),
        (x_far_now, x_near, blk_vals, w_base, other_tile),
        8,
    )
    far_1 = after((far_11, far_10))
    got_far_11, got_far_10 = swap(far_1[0], "feat", 2), swap(far_1[1], "feat", 2)
    got_near_11, got_near_01 = swap(near_11, "feat", 1), swap(near_01, "feat", 1)
    low = after(low)
    low = low + swap(low, "feat", 2)

    cot_seen = after(cot_seen)
    cot_own = [pick(cot_seen, turn)]
    for j in range(1, groups):
        cot_own.append(swap(pick(cot_seen, turn ^ j), "tok", 2 * j))
    g_near, g_far = joined(cot_own[:half_groups]), joined(cot_own[half_groups:])
    far_01 = added(far_01, after(got_far_11, g_near))
    got_far_01 = swap(far_01, "feat", 1)

    near_10 = added(near_10, after(got_near_11, far_01))
    got_near_10 = swap(near_10, "feat", 2)
    far_00 = added(far_00, after(got_far_10, near_10))
    near_00 = added(near_00, after(got_near_01, near_10))
    g_near = after(g_near, far_01)
    g_far = after(g_far, near_10)
    g_far_01, g_near_10 = swap(g_far, "feat", 1), swap(g_near, "feat", 2)
    g_near_01, g_far_10 = swap(g_near, "feat", 1), swap(g_far, "feat", 2)
    low = after(low, g_far)
    mask = 4
    while mask < lax.axis_size("feat"):
        low = low + swap(low, "feat", mask)
        mask *= 2
    far = added(far_00, after(got_far_01, g_near, g_far))

    parts = parted(far, far)
    got_parts = {j: swap(parts[j], "tok", 2 * j) for j in range(half_groups, groups)}
    near = added(near_00, after(got_near_10))
    g_near_11 = swap(after(g_near_10, near), "feat", 1)
    g_far_11 = swap(after(g_far_01), "feat", 2)
    parts = parted(near, far)
    got_parts.update({j: swap(parts[j], "tok", 2 * j) for j in range(1, half_groups)})
    parts = [parts[0]] + [got_parts[j] for j in range(1, groups)]
    total = pick(parts, turn).astype(F32)
    sent = [pick(parts, turn ^ step) for step in range(1, groups)]
    got_total = [swap(part, "feat", 4 * step) for step, part in enumerate(sent, 1)]
    low = after(low.astype(BF16))
    u_half, v_half = low[:, :rank], low[:, rank:]
    up = jnp.dot(u_half.T, grad_out, preferred_element_type=F32)
    up = (up + after(swap(up, "tok", 1))).astype(BF16)
    got_v = [swap(v_half, "tok", 2 * j) for j in range(1, groups)]
    v_groups = [v_half] + after(got_v, near)
    down = tree_sum(
        [jnp.dot(x.T, v, preferred_element_type=F32) for x, v in zip(x_groups, v_groups)]
    )

    short = (set_rows, shard)
    acc_near, acc_far, blocks, last_tile, vals_seen = call(
        early_kernel,
        20,
        1,
        [(short, F32)] * 2 + [(blk_vals.shape, F32), (tile_half, BF16), (blk_vals.shape, BF16)],
        [
            pltpu.VMEM((3, *tile_half), BF16),
            pltpu.VMEM(tall, BF16),
            pltpu.VMEM(tall, F32),
            pltpu.SemaphoreType.DMA((5,)),
        ],
        6 * product,
        scalars,
        (*x_pair, after(g_near), g_far, g_near_01, g_far_01, g_near_10, g_far_10),
        (blk_vals, w_base, other_tile),
    )
    piece = (tok_rows, shard)
    *rest_far, blocks = call(
        late_kernel,
        32,
        0.01,
        [(piece, BF16)] * half_groups + [(blk_vals.shape, F32)],
        [pltpu.VMEM(short, F32)],
        product,
        scalars,
        (x_far, after(g_far_11), acc_far, blocks, vals_seen, last_tile),
    )
    own, *rest, blocks = call(
        late_kernel,
        32,
        0.01,
        [(piece, F32)] + [(piece, BF16)] * (half_groups - 1) + [(blk_vals.shape, F32)],
        [pltpu.VMEM(short, F32)],
        product,
        scalars,
        (x_near, g_near_11, acc_near, blocks, vals_seen, last_tile),
    )
    rest = [*rest, *rest_far]
    rest = after(rest)
    got_rest = [swap(rest[j - 1], "tok", 2 * j) for j in range(1, groups)]

    blocks = blocks.astype(BF16)
    down = down + after(swap(down, "tok", 1))
    mask = 2
    while mask < n_tok:
        up = up.astype(F32) + after(swap(up.astype(BF16), "tok", mask)).astype(F32)
        blocks = blocks + swap(blocks, "tok", mask)
        mask *= 2
    blocks = blocks.astype(F32) + swap(blocks, "tok", 1).astype(F32)

    for got in got_total:
        total = total + got.astype(F32)
    projected = (total + jnp.dot(u_half, b_up, preferred_element_type=F32)).astype(BF16)
    for got in got_rest:
        own = own + got.astype(F32)
    grad_x = (own + jnp.dot(v_half, a_down.T, preferred_element_type=F32)).astype(BF16)
    return projected, grad_x, blocks * grad_scale, down * grad_scale, up * grad_scale


def solution(mesh):
    in_specs = (
        P("tok", "feat"),
        P("feat", "tok"),
        P("feat", None, None),
        P("feat", None),
        P("feat"),
        P("feat", None),
        P(None, "feat"),
        P("tok", "feat"),
    )
    out_specs = (
        P("tok", "feat"),
        P("tok", "feat"),
        P("feat", None, None),
        P("feat", None),
        P(None, "feat"),
    )
    return jax.shard_map(
        on_device, mesh=mesh, in_specs=in_specs, out_specs=out_specs, check_vma=False
    )
```
